32 devices in a mesh: tm: 4 (over y, x), space: 8 (over z, core).
Axes of the slice: x: 2, y: 2, z: 4, core: 2. Of those that a mesh axis runs over, the one named last changes fastest.
Arguments:
- starts: float32 [4, 64, 256, 128], P('tm', 'space'), may hold values from -6 to 6
- material: int32 [64, 256, 128], P('space'), may hold values from 0 to 7, as said below
- source: float32 [64, 256, 128], P('space'), may hold values from -6 to 6
Outputs:
- next_starts: float32 [4, 64, 256, 128], P('tm', 'space')
The draws below stay inside these ranges and needn't reach their ends.
Inputs may be any that keep to these rules, and one draw needn't show every extreme that they name: `material`: index into the table of 8 conductivities.
All inputs are finite; a program needn't handle non-finite values.
Results may differ from the reference program's by a relative error of at most 0.0001.
Values sent between devices are 32-bit elements; how exact they have to be, the bound alone decides.
A program may use at most 64 MiB of HBM per device.

```python
import jax
import jax.numpy as jnp

NY = 256
NZ = 128
FSTEPS = 4
CSTEPS = 2
ITERS = 1
NT = 4
NX = 64
N_TM = 4


def draw_material(key, part):
    key_base, key_pick, key_spot = jax.random.split(key, 3)
    shape = (NX, NY, NZ)
    total = NX * NY * NZ
    base = jax.random.randint(key_base, shape, 0, 8, dtype=jnp.int32)
    pick = jax.random.randint(key_pick, shape, 0, 8, dtype=jnp.int32)
    values = jnp.where(pick < 7, jnp.int32(0), base)
    spot = jax.random.randint(key_spot, (), 0, total - 1, dtype=jnp.int32)
    flat = jnp.arange(total, dtype=jnp.int32).reshape(shape)
    values = jnp.where(flat == spot, jnp.int32(7), values)
    values = jnp.where(flat == spot + 1, jnp.int32(0), values)
    return values.astype(jnp.int32)


def block_scale(own_key, shape, cuts, least, high):
    factor_of = 1.0
    for dim, blocks in cuts:
        heights = jax.random.uniform(jax.random.fold_in(jax.random.fold_in(own_key, 6), dim), (blocks,), jnp.float32, least / len(cuts), high / len(cuts))
        factor_of = factor_of * jnp.repeat(jnp.exp(heights), shape[dim] // blocks).reshape((-1,) + (1,) * (len(shape) - 1 - dim))
    return factor_of


def gaussian(rng, extent, scale, reach, pieces=(), kind=jnp.bfloat16):
    values = scale * jax.random.normal(rng, extent, jnp.float32)
    if pieces:
        values = values * block_scale(rng, extent, pieces, -0.22, 0.18)
    return jnp.clip(values, -reach, reach).astype(kind)


def setup_inputs(seed: int = 0) -> dict:
    seeds = jax.random.split(jax.random.key(seed), 4)
    return {
        "starts": gaussian(seeds[0], (NT, NX, NY, NZ), 1.0, 6.0, ((0, 4), (1, 8)), jnp.float32),
        "material": draw_material(jax.random.fold_in(seeds[3], 71), 0),
        "source": gaussian(seeds[2], (NX, NY, NZ), 1.0, 6.0, ((0, 8),), jnp.float32),
    }


conductivity_table = (1.0, 0.72, 0.52, 0.37, 0.26, 0.18, 0.13, 0.09)
fine_step = 0.15
coarse_step = 0.3


def lookup(material):
    result = jnp.zeros(material.shape, jnp.float32)
    for number in range(8):
        result = jnp.where(material == number, jnp.float32(conductivity_table[number]), result)
    return result


def restrict(values):
    lead_dims = values.shape[:-3]
    folded = values.reshape(lead_dims + (values.shape[-3] // 2, 2, values.shape[-2] // 2, 2, values.shape[-1]))
    return jnp.mean(folded, axis=(-4, -2))


def prolong(values):
    lead_dims = values.shape[:-3]
    rows_x = values.shape[-3]
    rows_y = values.shape[-2]
    rows_z = values.shape[-1]
    spread = jnp.broadcast_to(values[..., :, None, :, None, :], lead_dims + (rows_x, 2, rows_y, 2, rows_z))
    return spread.reshape(lead_dims + (rows_x * 2, rows_y * 2, rows_z))


def make_faces(cond_pad, weight_x, weight_y, weight_z):
    own = cond_pad[1:-1]
    face_x = weight_x * 0.5 * (cond_pad[1:] + cond_pad[:-1])
    pad_y = jnp.pad(own, ((0, 0), (1, 1), (0, 0)))
    face_y = weight_y * 0.5 * (pad_y[:, 1:] + pad_y[:, :-1])
    pad_z = jnp.pad(own, ((0, 0), (0, 0), (1, 1)))
    face_z = weight_z * 0.5 * (pad_z[:, :, 1:] + pad_z[:, :, :-1])
    return face_x, face_y, face_z


def diffuse(padded, face_x, face_y, face_z, source_in, step_size):
    current = padded[1:-1]
    grad_x = face_x * (padded[1:] - padded[:-1])
    flux = grad_x[1:] - grad_x[:-1]
    field_y = jnp.pad(current, ((0, 0), (1, 1), (0, 0)))
    grad_y = face_y * (field_y[:, 1:] - field_y[:, :-1])
    flux = flux + grad_y[:, 1:] - grad_y[:, :-1]
    field_z = jnp.pad(current, ((0, 0), (0, 0), (1, 1)))
    grad_z = face_z * (field_z[:, :, 1:] - field_z[:, :, :-1])
    flux = flux + grad_z[:, :, 1:] - grad_z[:, :, :-1]
    return current + step_size * (flux + source_in)


def xpad(values):
    return jnp.pad(values, ((1, 1), (0, 0), (0, 0)))


def reference(starts, material, source):
    conduct = lookup(material)
    fine_faces = make_faces(xpad(conduct), 1.0, 1.0, 1.0)
    coarse_faces = make_faces(xpad(restrict(conduct)), 0.25, 0.25, 1.0)
    coarse_source = restrict(source)

    def fine_run(current):
        for step_num in range(FSTEPS):
            current = diffuse(xpad(current), fine_faces[0], fine_faces[1], fine_faces[2], source, fine_step)
        return current

    def coarse_run(current):
        reduced = restrict(current)
        for step_num in range(CSTEPS):
            reduced = diffuse(xpad(reduced), coarse_faces[0], coarse_faces[1], coarse_faces[2], coarse_source, coarse_step)
        return prolong(reduced)

    slabs = [starts[slab_num] for slab_num in range(N_TM)]
    coarse_now = [coarse_run(slab_start) for slab_start in slabs]
    offsets = []
    for iter_num in range(ITERS):
        offsets = [fine_run(slabs[slab_num]) - coarse_now[slab_num] for slab_num in range(N_TM)]
        updated = [slabs[0]]
        for slab_num in range(N_TM - 1):
            updated.append(coarse_run(updated[slab_num]) + offsets[slab_num])
        slabs = updated
        coarse_now = [coarse_run(slab_start) for slab_start in slabs]
    newest = coarse_now[-1] + offsets[-1]
    return jnp.stack([newest] + slabs[1:])
```

```python
import functools

import jax
import jax.numpy as jnp
from jax import lax
from jax.experimental import pallas as pl
from jax.experimental.pallas import tpu as pltpu
from jax.sharding import PartitionSpec as P

FSTEPS = 4
CSTEPS = 2
PAD = 8
CHUNK = 64

conductivity_table = (1.0, 0.72, 0.52, 0.37, 0.26, 0.18, 0.13, 0.09)
fine_step = 0.15
coarse_step = 0.3

MESH = pl.DeviceIdType.MESH


def lookup(material):
    result = jnp.zeros(material.shape, jnp.float32)
    for number in range(8):
        result = jnp.where(material == number, jnp.float32(conductivity_table[number]), result)
    return result


def kernel(slabs, blocks, starts, material, source, out, ub, kb, wx, wyl, wyh, wzl, wzh, c0, hs, arrived,
           ru_pad, rf_pad, kc_pad, sc_pad, kcw, cw, gu, gu2, rb, rf, send_e, ec, tmp,
           load_sem, fs, fr, ks, kr, cs, cr, gs, gr, hs_sem, hr_sem, us, ur, vs, vr, es, er, bs, br):
    nx, ny, nz = out.shape
    ncx, ncy = nx // 2, ny // 2
    rows = ncy // slabs
    side = (kc_pad.shape[1] - ncy) // 2
    width = rows + 2 * side
    tm = lax.axis_index("tm")
    sp = lax.axis_index("space")
    has_low = sp > 0
    has_high = sp < blocks - 1
    pending = []

    def remote(cond, src, dst, send, recv, **where):
        copy = pltpu.make_async_remote_copy(
            src_ref=src, dst_ref=dst, send_sem=send, recv_sem=recv, device_id=where, device_id_type=MESH
        )

        @pl.when(cond)
        def _():
            copy.start()

        pending.append((cond, copy))

    def arrive(cond, dst, recv):
        copy = pltpu.make_async_remote_copy(
            src_ref=dst, dst_ref=dst, send_sem=recv, recv_sem=recv, device_id={"tm": tm}, device_id_type=MESH
        )

        @pl.when(cond)
        def _():
            copy.wait_recv()

    def halo(low_src, low_dst, high_src, high_dst, send, recv):
        remote(has_low, low_src, low_dst, send.at[0], recv.at[0], space=sp - 1)
        remote(has_high, high_src, high_dst, send.at[1], recv.at[1], space=sp + 1)

    def halo_wait(low_dst, high_dst, recv):
        arrive(has_high, low_dst, recv.at[0])
        arrive(has_low, high_dst, recv.at[1])

    barrier = pltpu.get_barrier_semaphore()

    @pl.when(has_low)
    def _():
        pl.semaphore_signal(barrier, inc=1, device_id={"space": sp - 1}, device_id_type=MESH)

    @pl.when(has_high)
    def _():
        pl.semaphore_signal(barrier, inc=1, device_id={"space": sp + 1}, device_id_type=MESH)

    for by in range(1, slabs):
        pl.semaphore_signal(barrier, inc=1, device_id={"tm": lax.rem(tm + by, slabs)}, device_id_type=MESH)

    load = pltpu.make_async_copy(starts.at[0], ub.at[0, pl.ds(1, nx), pl.ds(PAD, ny)], load_sem)
    load.start()

    strip = jnp.zeros((PAD, nz), jnp.float32)

    def clear_rows(plane, carry):
        for step in range(FSTEPS):
            ub[step, plane, 0:PAD] = strip
            ub[step, plane, PAD + ny:PAD + ny + PAD] = strip
        kb[plane, 0:PAD] = strip
        kb[plane, PAD + ny:PAD + ny + PAD] = strip
        return carry

    lax.fori_loop(1, nx + 1, clear_rows, 0)
    for ref in (ru_pad, rf_pad, kc_pad, sc_pad):
        for plane in range(ncx):
            ref[plane, 0:side] = jnp.zeros((side, nz), jnp.float32)
            ref[plane, side + ncy:side + ncy + side] = jnp.zeros((side, nz), jnp.float32)

    def clear_ghosts(fine, coarse):
        for step in range(FSTEPS):
            ub[step, fine, PAD:PAD + ny] = jnp.zeros((ny, nz), jnp.float32)
        kb[fine, PAD:PAD + ny] = jnp.zeros((ny, nz), jnp.float32)
        blank = jnp.zeros((width, nz), jnp.float32)
        kcw[coarse] = blank
        for step in range(CSTEPS):
            for slab in range(slabs - 1):
                gu[step, slab, coarse] = blank
                rb[step, slab, coarse] = blank

    @pl.when(jnp.logical_not(has_low))
    def _():
        clear_ghosts(0, 0)

    @pl.when(jnp.logical_not(has_high))
    def _():
        clear_ghosts(nx + 1, ncx + 1)

    def conduct(plane):
        for at in range(0, ny, CHUNK):
            kb[plane + 1, PAD + at:PAD + at + CHUNK] = lookup(material[plane, at:at + CHUNK])

    conduct(0)
    conduct(nx - 1)

    pl.semaphore_wait(barrier, slabs - 1 + has_low.astype(jnp.int32) + has_high.astype(jnp.int32))

    inner = pl.ds(PAD, ny)
    halo(kb.at[1, inner], kb.at[nx + 1, inner], kb.at[nx, inner], kb.at[0, inner], ks, kr)
    load.wait()

    def send_fine(step):
        halo(ub.at[step, 1, inner], ub.at[step, nx + 1, inner], ub.at[step, nx, inner], ub.at[step, 0, inner],
             fs.at[step], fr.at[step])

    def wait_fine(step):
        halo_wait(ub.at[step, nx + 1, inner], ub.at[step, 0, inner], fr.at[step])

    send_fine(0)

    def restrict_plane(pick, plane, base):
        total = pick(2 * plane, base) + pick(2 * plane, base + 1)
        return (total + pick(2 * plane + 1, base) + pick(2 * plane + 1, base + 1)) * 0.25

    def restrict_into(pad_ref, pick, base, scale=1.0):
        for plane in range(ncx):
            value = restrict_plane(pick, plane, base)
            pad_ref[plane, side:side + ncy] = value * scale if scale != 1.0 else value

    restrict_into(ru_pad, lambda plane, at: ub[0, plane + 1, pl.ds(at, ncy, stride=2)], PAD)

    def strip_of(ref, number):
        return ref.at[:, pl.ds(rows * number, width)]

    for to in range(slabs):
        remote(jnp.logical_and(tm != to, tm > 0), strip_of(ru_pad, to),
               gu.at[0, jnp.maximum(tm - 1, 0), pl.ds(1, ncx)], us.at[to], ur.at[tm], tm=to)

    def conduct_loop(plane, carry):
        conduct(plane)
        return carry

    lax.fori_loop(1, nx - 1, conduct_loop, 0)
    restrict_into(kc_pad, lambda plane, at: kb[plane + 1, pl.ds(at, ncy, stride=2)], PAD)
    restrict_into(sc_pad, lambda plane, at: source[plane, pl.ds(at, ncy, stride=2)], 0, coarse_step)
    mine = pl.ds(pl.multiple_of(rows * tm, 8), width)
    for plane in range(ncx):
        kcw[plane + 1] = kc_pad[plane, mine]
    halo(kcw.at[1], kcw.at[ncx + 1], kcw.at[ncx], kcw.at[0], cs, cr)

    def fine_weights(plane):
        half = 0.5 * fine_step
        for at in range(0, ny, CHUNK):
            r = slice(PAD + at, PAD + at + CHUNK)
            q = slice(at, at + CHUNK)
            k = kb[plane + 1, r]
            lane = lax.broadcasted_iota(jnp.int32, k.shape, 1)
            x_low = half * (k + kb[plane, r])
            x_high = half * (k + kb[plane + 2, r])
            y_low = half * (k + kb[plane + 1, PAD + at - 1:PAD + at - 1 + CHUNK])
            y_high = half * (k + kb[plane + 1, PAD + at + 1:PAD + at + 1 + CHUNK])
            first, last = lane == 0, lane == nz - 1
            z_low = half * (k + jnp.where(first, 0.0, pltpu.roll(k, 1, 1)))
            z_high = half * (k + jnp.where(last, 0.0, pltpu.roll(k, nz - 1, 1)))
            wx[plane, q] = x_low
            wx[plane + 1, q] = x_high
            wyl[plane, q] = y_low
            wyh[plane, q] = y_high
            wzl[plane, q] = jnp.where(first, 0.0, z_low)
            wzh[plane, q] = jnp.where(last, 0.0, z_high)
            c0[plane, q] = 1.0 - (x_low + x_high + y_low + y_high + z_low + z_high)
            hs[plane, q] = fine_step * source[plane, q]

    def weights_loop(plane, carry):
        fine_weights(plane)
        return carry

    lax.fori_loop(1, nx - 1, weights_loop, 0)
    halo_wait(kb.at[nx + 1, inner], kb.at[0, inner], kr)
    fine_weights(0)
    fine_weights(nx - 1)

    def fine_plane(step, plane):
        for at in range(0, ny, CHUNK):
            r = slice(PAD + at, PAD + at + CHUNK)
            q = slice(at, at + CHUNK)
            u = ub[step, plane + 1, r]
            total = c0[plane, q] * u + hs[plane, q]
            total += wx[plane, q] * ub[step, plane, r]
            total += wx[plane + 1, q] * ub[step, plane + 2, r]
            total += wyl[plane, q] * ub[step, plane + 1, PAD + at - 1:PAD + at - 1 + CHUNK]
            total += wyh[plane, q] * ub[step, plane + 1, PAD + at + 1:PAD + at + 1 + CHUNK]
            total += wzl[plane, q] * pltpu.roll(u, 1, 1)
            total += wzh[plane, q] * pltpu.roll(u, nz - 1, 1)
            ub[step + 1, plane + 1, r] = total

    def coarse_weights():
        halo_wait(kcw.at[ncx + 1], kcw.at[0], cr)
        half = 0.5 * coarse_step
        near = 0.25 * half
        shape = (width, nz)
        lane = lax.broadcasted_iota(jnp.int32, shape, 1)
        row = lax.broadcasted_iota(jnp.int32, shape, 0) + (rows * tm - side)
        first, last = lane == 0, lane == nz - 1
        low_in = jnp.logical_and(row >= 1, row < ncy)
        high_in = jnp.logical_and(row >= 0, row < ncy - 1)
        for plane in range(ncx):
            k = kcw[plane + 1]
            x_low = near * (k + kcw[plane])
            x_high = near * (k + kcw[plane + 2])
            y_low = near * (k + pltpu.roll(k, 1, 0))
            y_high = near * (k + pltpu.roll(k, width - 1, 0))
            z_low = half * (k + jnp.where(first, 0.0, pltpu.roll(k, 1, 1)))
            z_high = half * (k + jnp.where(last, 0.0, pltpu.roll(k, nz - 1, 1)))
            cw[0, plane] = 1.0 - (x_low + x_high + y_low + y_high + z_low + z_high)
            cw[1, plane] = x_low
            cw[2, plane] = x_high
            cw[3, plane] = jnp.where(low_in, y_low, 0.0)
            cw[4, plane] = jnp.where(high_in, y_high, 0.0)
            cw[5, plane] = jnp.where(first, 0.0, z_low)
            cw[6, plane] = jnp.where(last, 0.0, z_high)
            cw[7, plane] = sc_pad[plane, mine]

    def coarse_plane(ref, step, slab, plane):
        v = ref[step, slab, plane + 1]
        total = cw[0, plane] * v + cw[7, plane]
        total += cw[1, plane] * ref[step, slab, plane]
        total += cw[2, plane] * ref[step, slab, plane + 2]
        total += cw[3, plane] * pltpu.roll(v, 1, 0)
        total += cw[4, plane] * pltpu.roll(v, width - 1, 0)
        total += cw[5, plane] * pltpu.roll(v, 1, 1)
        total += cw[6, plane] * pltpu.roll(v, nz - 1, 1)
        return total

    def send_start(step):
        halo(gu.at[step, :, 1], gu.at[step, :, ncx + 1], gu.at[step, :, ncx], gu.at[step, :, 0],
             gs.at[step], gr.at[step])

    def wait_start(step):
        halo_wait(gu.at[step, :, ncx + 1], gu.at[step, :, 0], gr.at[step])

    def coarse_starts(stage):
        if stage == 0:
            for slab in range(1, slabs):
                arrive(tm != slab, gu.at[0, slab - 1, pl.ds(1, ncx)], ur.at[slab])

                @pl.when(tm == slab)
                def _():
                    for plane in range(ncx):
                        gu[0, slab - 1, plane + 1] = ru_pad[plane, mine]

            send_start(0)
            coarse_weights()
        elif stage == 1:
            wait_start(0)
            for slab in range(slabs - 1):
                for plane in range(ncx):
                    gu[1, slab, plane + 1] = coarse_plane(gu, 0, slab, plane)
            send_start(1)
        elif stage == 2:
            wait_start(1)
            for slab in range(slabs - 1):
                for plane in range(ncx):
                    gu2[slab, plane] = coarse_plane(gu, 1, slab, plane)

    for step in range(FSTEPS):
        wait_fine(step)
        fine_plane(step, 0)
        fine_plane(step, nx - 1)
        if step < FSTEPS - 1:
            send_fine(step + 1)

        def fine_loop(plane, carry, step=step):
            fine_plane(step, plane)
            return carry

        lax.fori_loop(1, nx - 1, fine_loop, 0)
        coarse_starts(step)

    restrict_into(rf_pad, lambda plane, at: ub[FSTEPS, plane + 1, pl.ds(at, ncy, stride=2)], PAD)
    for to in range(slabs):
        remote(jnp.logical_and(tm != to, tm < slabs - 1), strip_of(rf_pad, to),
               rf.at[jnp.minimum(tm, slabs - 2)], vs.at[to], vr.at[tm], tm=to)
    for pair in range(ncx):
        remote(True, ub.at[FSTEPS, pl.ds(2 * pair + 1, 2), inner], arrived.at[pl.ds(2 * pair, 2)],
               bs.at[pair], br.at[pair], tm=lax.rem(tm + 1, slabs))

    def end_state(slab):
        arrive(tm != slab, rf.at[slab], vr.at[slab])

        @pl.when(tm == slab)
        def _():
            for plane in range(ncx):
                rf[slab, plane] = rf_pad[plane, mine]

    end_state(0)
    for plane in range(ncx):
        rb[0, 0, plane + 1] = rf[0, plane]
    for slab in range(1, slabs):
        at = slab - 1
        for step in range(CSTEPS):
            number = at * CSTEPS + step
            halo(rb.at[step, at, 1], rb.at[step, at, ncx + 1], rb.at[step, at, ncx], rb.at[step, at, 0],
                 hs_sem.at[number], hr_sem.at[number])
            if step == 0 and slab < slabs - 1:
                end_state(slab)
            halo_wait(rb.at[step, at, ncx + 1], rb.at[step, at, 0], hr_sem.at[number])
            for plane in range(ncx):
                value = coarse_plane(rb, step, at, plane)
                if step < CSTEPS - 1:
                    rb[step + 1, at, plane + 1] = value
                else:
                    value = value - gu2[at, plane]
                    send_e[at, plane] = value
                    if slab < slabs - 1:
                        rb[0, at + 1, plane + 1] = value + rf[slab, plane]
        to = (slab + 1) % slabs
        keep = pl.ds(side, rows)
        remote(tm != to, send_e.at[at, :, keep], ec.at[:, pl.ds(pl.multiple_of(rows * tm, 8), rows)],
               es.at[at], er.at[tm], tm=to)

        @pl.when(tm == to)
        def _():
            for plane in range(ncx):
                ec[plane, pl.ds(pl.multiple_of(rows * tm, 8), rows)] = send_e[at, plane, side:side + rows]

    @pl.when(tm == 1)
    def _():
        for plane in range(ncx):
            ec[plane] = jnp.zeros((ncy, nz), jnp.float32)

    for by in range(slabs):
        arrive(jnp.logical_and(tm != 1, tm != by), ec.at[:, pl.ds(rows * by, rows)], er.at[by])
    for plane in range(ncx):
        value = ec[plane]
        tmp[plane, pl.ds(0, ncy, stride=2)] = value
        tmp[plane, pl.ds(1, ncy, stride=2)] = value
    for pair in range(ncx):
        arrive(True, arrived.at[pl.ds(2 * pair, 2)], br.at[pair])
        for at in range(0, ny, CHUNK):
            q = slice(at, at + CHUNK)
            out[2 * pair, q] = arrived[2 * pair, q] + tmp[pair, q]
            out[2 * pair + 1, q] = arrived[2 * pair + 1, q] + tmp[pair, q]
    for cond, copy in pending:
        @pl.when(cond)
        def _(copy=copy):
            copy.wait_send()


def local(starts, material, source):
    slabs = lax.axis_size("tm")
    blocks = lax.axis_size("space")
    nx, ny, nz = source.shape
    ncx, ncy = nx // 2, ny // 2
    side = -(-CSTEPS * (slabs - 1) // 8) * 8
    width = ncy // slabs + 2 * side
    f32 = functools.partial(pltpu.VMEM, dtype=jnp.float32)
    sems = lambda *shape: pltpu.SemaphoreType.DMA(shape)
    field = (nx, ny, nz)
    padded = (ncx, ncy + 2 * side, nz)
    live = slabs - 1
    scratch = [
        f32((FSTEPS + 1, nx + 2, ny + 2 * PAD, nz)),
        f32((nx + 2, ny + 2 * PAD, nz)),
        f32((nx + 1, ny, nz)),
        *[f32(field) for _ in range(7)],
        *[f32(padded) for _ in range(4)],
        f32((ncx + 2, width, nz)),
        f32((8, ncx, width, nz)),
        f32((CSTEPS, live, ncx + 2, width, nz)),
        f32((live, ncx, width, nz)),
        f32((CSTEPS, live, ncx + 2, width, nz)),
        f32((live, ncx, width, nz)),
        f32((live, ncx, width, nz)),
        f32((ncx, ncy, nz)),
        f32((ncx, ny, nz)),
        pltpu.SemaphoreType.DMA,
        sems(FSTEPS, 2), sems(FSTEPS, 2),
        sems(2), sems(2),
        sems(2), sems(2),
        sems(CSTEPS, 2), sems(CSTEPS, 2),
        sems(live * CSTEPS, 2), sems(live * CSTEPS, 2),
        sems(slabs), sems(slabs),
        sems(slabs), sems(slabs),
        sems(slabs), sems(slabs),
        sems(ncx), sems(ncx),
    ]
    vmem = pl.BlockSpec(memory_space=pltpu.VMEM)
    result = pl.pallas_call(
        functools.partial(kernel, slabs, blocks),
        out_shape=jax.ShapeDtypeStruct(field, jnp.float32),
        in_specs=[pl.BlockSpec(memory_space=pl.ANY), vmem, vmem],
        out_specs=vmem,
        scratch_shapes=scratch,
        compiler_params=pltpu.CompilerParams(
            collective_id=0, has_side_effects=True, vmem_limit_bytes=48 * 1024 * 1024
        ),
    )(starts, material, source)
    return result[None]


def solution(mesh):
    in_specs = (P("tm", "space", None, None), P("space", None, None), P("space", None, None))
    out_specs = P("tm", "space", None, None)
    return jax.shard_map(local, mesh=mesh, in_specs=in_specs, out_specs=out_specs, check_vma=False)
```

```python
import functools

import jax
import jax.numpy as jnp
from jax import lax
from jax.experimental import pallas as pl
from jax.experimental.pallas import tpu as pltpu
from jax.sharding import PartitionSpec as P

FSTEPS = 4
CSTEPS = 2
PAD = 8
CHUNK = 64

conductivity_table = (1.0, 0.72, 0.52, 0.37, 0.26, 0.18, 0.13, 0.09)
fine_step = 0.15
coarse_step = 0.3

MESH = pl.DeviceIdType.MESH


def lookup(material):
    result = jnp.zeros(material.shape, jnp.float32)
    for number in range(8):
        result = jnp.where(material == number, jnp.float32(conductivity_table[number]), result)
    return result


def kernel(slabs, blocks, starts, material, source, out, mat, src, ub, ub2, kb, wx, wyl, wyh, wzl, wzh, c0, hs, full,
           kcb, cw, rub, rum, delta, rb, rm, got, last_state, ec, tmp, load_sem,
           fs, fr, f2s, f2r, ks, kr, cs, cr, chs, chr_, us, ur, vs, vr, es, er, bs, br):
    nx, ny, nz = src.shape
    ncx, ncy = nx // 2, ny // 2
    early = ub2.shape[2] - 2 * PAD
    whole = kcb.shape[1]
    side = (whole - ncy) // 2
    rows = ncy // slabs
    width = rows + 2 * side
    late = early - 8
    live = slabs - 1
    tm = lax.axis_index("tm")
    sp = lax.axis_index("space")
    has_low = sp > 0
    has_high = sp < blocks - 1
    after = lax.rem(tm + 1, slabs)
    pending = []

    def remote(cond, src_ref, dst_ref, send, recv, **where):
        copy = pltpu.make_async_remote_copy(
            src_ref=src_ref, dst_ref=dst_ref, send_sem=send, recv_sem=recv, device_id=where, device_id_type=MESH
        )

        @pl.when(cond)
        def _():
            copy.start()

        pending.append((cond, copy))

    def arrive(cond, dst_ref, recv):
        copy = pltpu.make_async_remote_copy(
            src_ref=dst_ref, dst_ref=dst_ref, send_sem=recv, recv_sem=recv, device_id={"tm": tm}, device_id_type=MESH
        )

        @pl.when(cond)
        def _():
            copy.wait_recv()

    def halo(low_src, low_dst, high_src, high_dst, send, recv):
        remote(has_low, low_src, low_dst, send.at[0], recv.at[0], space=sp - 1)
        remote(has_high, high_src, high_dst, send.at[1], recv.at[1], space=sp + 1)

    def halo_wait(low_dst, high_dst, recv):
        arrive(has_high, low_dst, recv.at[0])
        arrive(has_low, high_dst, recv.at[1])

    barrier = pltpu.get_barrier_semaphore()

    @pl.when(has_low)
    def _():
        pl.semaphore_signal(barrier, inc=1, device_id={"space": sp - 1}, device_id_type=MESH)

    @pl.when(has_high)
    def _():
        pl.semaphore_signal(barrier, inc=1, device_id={"space": sp + 1}, device_id_type=MESH)

    for by in range(1, slabs):
        pl.semaphore_signal(barrier, inc=1, device_id={"tm": lax.rem(tm + by, slabs)}, device_id_type=MESH)

    load_mat = pltpu.make_async_copy(material, mat, load_sem.at[0])
    load_mat.start()
    load_u = pltpu.make_async_copy(starts.at[0], ub.at[0, pl.ds(1, nx), pl.ds(PAD, ny)], load_sem.at[1])
    load_u.start()
    load_src = pltpu.make_async_copy(source, src, load_sem.at[2])
    load_src.start()

    strip = jnp.zeros((PAD, nz), jnp.float32)

    def clear_rows(plane, carry):
        for step in range(FSTEPS):
            ub[step, plane, 0:PAD] = strip
            ub[step, plane, PAD + ny:PAD + ny + PAD] = strip
            ub2[step, plane, 0:PAD] = strip
            ub2[step, plane, PAD + early:PAD + early + PAD] = strip
        kb[plane, 0:PAD] = strip
        kb[plane, PAD + ny:PAD + ny + PAD] = strip
        return carry

    lax.fori_loop(1, nx + 1, clear_rows, 0)
    edge = jnp.zeros((side, nz), jnp.float32)

    def clear_sides(plane, carry):
        for ref in (kcb, rub):
            ref[plane, 0:side] = edge
            ref[plane, side + ncy:whole] = edge
        return carry

    lax.fori_loop(0, ncx + 4, clear_sides, 0)
    for plane in range(ncx + 2):
        cw[7, plane, 0:side] = edge
        cw[7, plane, side + ncy:whole] = edge
    for plane in range(ncx):
        delta[plane, 0:side] = edge
        delta[plane, side + ncy:whole] = edge

    def clear_ghosts(fine, coarse):
        for step in range(FSTEPS):
            ub[step, fine, PAD:PAD + ny] = jnp.zeros((ny, nz), jnp.float32)
            ub2[step, fine, PAD:PAD + early] = jnp.zeros((early, nz), jnp.float32)
        kb[fine, PAD:PAD + ny] = jnp.zeros((ny, nz), jnp.float32)
        for plane in (coarse, coarse + 1):
            kcb[plane] = jnp.zeros((whole, nz), jnp.float32)
            rub[plane] = jnp.zeros((whole, nz), jnp.float32)
            for slab in range(live):
                rb[slab, plane] = jnp.zeros((width, nz), jnp.float32)

    @pl.when(jnp.logical_not(has_low))
    def _():
        clear_ghosts(0, 0)
        cw[7, 0] = jnp.zeros((whole, nz), jnp.float32)

    @pl.when(jnp.logical_not(has_high))
    def _():
        clear_ghosts(nx + 1, ncx + 2)
        cw[7, ncx + 1] = jnp.zeros((whole, nz), jnp.float32)

    def conduct(plane):
        for at in range(0, ny, CHUNK):
            kb[plane + 1, PAD + at:PAD + at + CHUNK] = lookup(mat[plane, at:at + CHUNK])

    load_mat.wait()
    conduct(0)
    conduct(nx - 1)
    pl.semaphore_wait(barrier, slabs - 1 + has_low.astype(jnp.int32) + has_high.astype(jnp.int32))

    inner = pl.ds(PAD, ny)
    first_rows = pl.ds(PAD, early)
    halo(starts.at[0, 0], ub.at[0, nx + 1, inner], starts.at[0, nx - 1], ub.at[0, 0, inner], fs.at[0], fr.at[0])
    halo(kb.at[1, inner], kb.at[nx + 1, inner], kb.at[nx, inner], kb.at[0, inner], ks, kr)
    for pair in range(ncx):
        remote(True, starts.at[0, pl.ds(2 * pair, 2), pl.ds(0, early)],
               ub2.at[0, pl.ds(2 * pair + 1, 2), first_rows], us.at[pair], ur.at[pair], tm=after)

    def send_fine(step):
        halo(ub.at[step, 1, inner], ub.at[step, nx + 1, inner], ub.at[step, nx, inner], ub.at[step, 0, inner],
             fs.at[step], fr.at[step])

    def wait_fine(step):
        halo_wait(ub.at[step, nx + 1, inner], ub.at[step, 0, inner], fr.at[step])

    def send_early(step):
        halo(ub2.at[step, 1, first_rows], ub2.at[step, nx + 1, first_rows],
             ub2.at[step, nx, first_rows], ub2.at[step, 0, first_rows], f2s.at[step], f2r.at[step])

    def wait_early(step):
        halo_wait(ub2.at[step, nx + 1, first_rows], ub2.at[step, 0, first_rows], f2r.at[step])

    def conduct_loop(plane, carry):
        conduct(plane)
        return carry

    lax.fori_loop(1, nx - 1, conduct_loop, 0)

    load_src.wait()

    def fine_weights(plane):
        half = 0.5 * fine_step
        for at in range(0, ny, CHUNK):
            r = slice(PAD + at, PAD + at + CHUNK)
            q = slice(at, at + CHUNK)
            k = kb[plane + 1, r]
            lane = lax.broadcasted_iota(jnp.int32, k.shape, 1)
            x_low = half * (k + kb[plane, r])
            x_high = half * (k + kb[plane + 2, r])
            y_low = half * (k + kb[plane + 1, PAD + at - 1:PAD + at - 1 + CHUNK])
            y_high = half * (k + kb[plane + 1, PAD + at + 1:PAD + at + 1 + CHUNK])
            first, last = lane == 0, lane == nz - 1
            z_low = half * (k + jnp.where(first, 0.0, pltpu.roll(k, 1, 1)))
            z_high = half * (k + jnp.where(last, 0.0, pltpu.roll(k, nz - 1, 1)))
            wx[plane, q] = x_low
            wx[plane + 1, q] = x_high
            wyl[plane, q] = y_low
            wyh[plane, q] = y_high
            wzl[plane, q] = jnp.where(first, 0.0, z_low)
            wzh[plane, q] = jnp.where(last, 0.0, z_high)
            c0[plane, q] = 1.0 - (x_low + x_high + y_low + y_high + z_low + z_high)
            hs[plane, q] = fine_step * src[plane, q]

    def weights_loop(plane, carry):
        fine_weights(plane)
        return carry

    lax.fori_loop(1, nx - 1, weights_loop, 0)
    halo_wait(kb.at[nx + 1, inner], kb.at[0, inner], kr)
    fine_weights(0)
    fine_weights(nx - 1)
    load_u.wait()

    def fine_plane(ref, plane, count, store):
        for at in range(0, count, CHUNK):
            size = min(CHUNK, count - at)
            q = slice(at, at + size)
            r = slice(PAD + at, PAD + at + size)
            u = ref[plane + 1, r]
            total = c0[plane, q] * u + hs[plane, q]
            total += wx[plane, q] * ref[plane, r]
            total += wx[plane + 1, q] * ref[plane + 2, r]
            total += wyl[plane, q] * ref[plane + 1, PAD + at - 1:PAD + at - 1 + size]
            total += wyh[plane, q] * ref[plane + 1, PAD + at + 1:PAD + at + 1 + size]
            total += wzl[plane, q] * pltpu.roll(u, 1, 1)
            total += wzh[plane, q] * pltpu.roll(u, nz - 1, 1)
            store(plane, at, size, total)

    def sweep(ref, count, store, send):
        fine_plane(ref, 0, count, store)
        fine_plane(ref, nx - 1, count, store)
        send()

        def fine_loop(plane, carry):
            fine_plane(ref, plane, count, store)
            return carry

        lax.fori_loop(1, nx - 1, fine_loop, 0)

    def into(ref):
        def store(plane, at, size, value):
            ref[plane + 1, PAD + at:PAD + at + size] = value
        return store

    def restrict_plane(ref, plane, base):
        total = ref[plane, pl.ds(base, ncy, stride=2)] + ref[plane, pl.ds(base + 1, ncy, stride=2)]
        total += ref[plane + 1, pl.ds(base, ncy, stride=2)]
        total += ref[plane + 1, pl.ds(base + 1, ncy, stride=2)]
        return total * 0.25

    core = slice(side, side + ncy)
    mid = pl.ds(side, ncy)

    def coarse_inputs():
        for plane in range(ncx):
            rub[plane + 2, core] = restrict_plane(ub.at[0], 2 * plane + 1, PAD)
            kcb[plane + 2, core] = restrict_plane(kb, 2 * plane + 1, PAD)
            cw[7, plane + 1, core] = coarse_step * restrict_plane(src, 2 * plane, 0)
        low, high = pl.ds(2, 2), pl.ds(ncx, 2)
        low_ghost, high_ghost = pl.ds(0, 2), pl.ds(ncx + 2, 2)
        halo(kcb.at[low, mid], kcb.at[high_ghost, mid], kcb.at[high, mid], kcb.at[low_ghost, mid], cs.at[0], cr.at[0])
        halo(rub.at[low, mid], rub.at[high_ghost, mid], rub.at[high, mid], rub.at[low_ghost, mid], cs.at[1], cr.at[1])
        halo(cw.at[7, 1, mid], cw.at[7, ncx + 1, mid], cw.at[7, ncx, mid], cw.at[7, 0, mid], cs.at[2], cr.at[2])

    def coarse_weights():
        low_ghost, high_ghost = pl.ds(0, 2), pl.ds(ncx + 2, 2)
        halo_wait(kcb.at[high_ghost, mid], kcb.at[low_ghost, mid], cr.at[0])
        halo_wait(rub.at[high_ghost, mid], rub.at[low_ghost, mid], cr.at[1])
        halo_wait(cw.at[7, ncx + 1, mid], cw.at[7, 0, mid], cr.at[2])
        half = 0.5 * coarse_step
        near = 0.25 * half
        shape = (whole, nz)
        lane = lax.broadcasted_iota(jnp.int32, shape, 1)
        row = lax.broadcasted_iota(jnp.int32, shape, 0) - side
        first, last = lane == 0, lane == nz - 1
        low_in = jnp.logical_and(row >= 1, row < ncy)
        high_in = jnp.logical_and(row >= 0, row < ncy - 1)
        for plane in range(ncx + 2):
            k = kcb[plane + 1]
            x_low = near * (k + kcb[plane])
            x_high = near * (k + kcb[plane + 2])
            y_low = near * (k + pltpu.roll(k, 1, 0))
            y_high = near * (k + pltpu.roll(k, whole - 1, 0))
            z_low = half * (k + jnp.where(first, 0.0, pltpu.roll(k, 1, 1)))
            z_high = half * (k + jnp.where(last, 0.0, pltpu.roll(k, nz - 1, 1)))
            cw[0, plane] = 1.0 - (x_low + x_high + y_low + y_high + z_low + z_high)
            cw[1, plane] = jnp.where(has_high, x_low, 0.0) if plane == ncx + 1 else x_low
            cw[2, plane] = jnp.where(has_low, x_high, 0.0) if plane == 0 else x_high
            cw[3, plane] = jnp.where(low_in, y_low, 0.0)
            cw[4, plane] = jnp.where(high_in, y_high, 0.0)
            cw[5, plane] = jnp.where(first, 0.0, z_low)
            cw[6, plane] = jnp.where(last, 0.0, z_high)

    def coarse_plane(ref, plane, pick, offset):
        v = ref[plane + 1]
        at = plane + offset
        total = cw[0, at, pick] * v + cw[7, at, pick]
        total += cw[1, at, pick] * ref[plane]
        total += cw[2, at, pick] * ref[plane + 2]
        total += cw[3, at, pick] * pltpu.roll(v, 1, 0)
        total += cw[4, at, pick] * pltpu.roll(v, v.shape[0] - 1, 0)
        total += cw[5, at, pick] * pltpu.roll(v, 1, 1)
        total += cw[6, at, pick] * pltpu.roll(v, nz - 1, 1)
        return total

    def coarse_map(ref, middle, pick, store):
        for plane in range(ncx + 2):
            middle[plane] = coarse_plane(ref, plane, pick, 0)
        for plane in range(ncx):
            store(plane, coarse_plane(middle, plane, pick, 1))

    for step in range(FSTEPS):
        wait_fine(step)

        def send(step=step):
            if step < FSTEPS - 1:
                send_fine(step + 1)

        sweep(ub.at[step], ny, into(ub.at[step + 1]), send)
        if step == 0:
            coarse_inputs()
        if step == FSTEPS - 2:
            coarse_weights()

            def keep_minus(plane, value):
                delta[plane] = jnp.where(tm > 0, -value, 0.0)

            coarse_map(rub, rum, slice(0, whole), keep_minus)

    for plane in range(ncx):
        delta[plane, core] = delta[plane, core] + restrict_plane(ub.at[FSTEPS], 2 * plane + 1, PAD)
    for to in range(slabs):
        remote(tm != to, delta.at[:, pl.ds(rows * to, width)], got.at[tm], vs.at[to], vr.at[tm], tm=to)
    for pair in range(ncx):
        remote(True, ub.at[FSTEPS, pl.ds(2 * pair + 1, 2), pl.ds(PAD + late, ny - late)],
               full.at[pl.ds(2 * pair, 2), pl.ds(late, ny - late)], bs.at[pair], br.at[pair], tm=after)

    mine = pl.ds(pl.multiple_of(rows * tm, 8), width)

    def end_state(slab):
        arrive(tm != slab, got.at[slab], vr.at[slab])

        @pl.when(tm == slab)
        def _():
            for plane in range(ncx):
                got[slab, plane] = delta[plane, mine]

    def send_chain(slab):
        halo(rb.at[slab, pl.ds(2, 2)], rb.at[slab, pl.ds(ncx + 2, 2)], rb.at[slab, pl.ds(ncx, 2)],
             rb.at[slab, pl.ds(0, 2)], chs.at[slab], chr_.at[slab])

    own_rows = pl.ds(pl.multiple_of(rows * tm, 8), rows)

    def chain(slab):
        end_state(slab + 1)
        halo_wait(rb.at[slab, pl.ds(ncx + 2, 2)], rb.at[slab, pl.ds(0, 2)], chr_.at[slab])
        to = (slab + 2) % slabs

        if slab + 1 < live:
            def store(plane, value):
                rb[slab + 1, plane + 2] = value + got[slab + 1, plane]

            coarse_map(rb.at[slab], rm, mine, store)
            send_chain(slab + 1)
            result = rb.at[slab + 1, pl.ds(2, ncx)]
        else:
            def store(plane, value):
                last_state[plane] = value + got[slab + 1, plane]

            coarse_map(rb.at[slab], rm, mine, store)
            result = last_state
        remote(tm != to, result.at[:, pl.ds(side, rows)], ec.at[:, own_rows], es.at[slab], er.at[tm], tm=to)

        @pl.when(tm == to)
        def _():
            for plane in range(ncx):
                ec[plane, own_rows] = result[plane, side:side + rows]

    for pair in range(ncx):
        arrive(True, ub2.at[0, pl.ds(2 * pair + 1, 2), first_rows], ur.at[pair])
    send_early(0)

    def early_step(step):
        wait_early(step)
        if step < FSTEPS - 1:
            sweep(ub2.at[step], early, into(ub2.at[step + 1]), lambda: send_early(step + 1))
        else:
            def store(plane, at, size, value):
                full[plane, at:at + size] = value

            sweep(ub2.at[step], late, store, lambda: None)

    early_step(0)
    end_state(0)
    for plane in range(ncx):
        rb[0, plane + 2] = got[0, plane]
    send_chain(0)
    for turn in range(max(FSTEPS - 1, live)):
        if turn + 1 < FSTEPS:
            early_step(turn + 1)
        if turn < live:
            chain(turn)

    @pl.when(tm == 1)
    def _():
        for plane in range(ncx):
            ec[plane] = jnp.zeros((ncy, nz), jnp.float32)

    for by in range(slabs):
        arrive(jnp.logical_and(tm != 1, tm != by), ec.at[:, pl.ds(rows * by, rows)], er.at[by])
    for pair in range(ncx):
        arrive(True, full.at[pl.ds(2 * pair, 2), pl.ds(late, ny - late)], br.at[pair])
        value = ec[pair] - restrict_plane(full, 2 * pair, 0)
        value = jnp.where(tm == 1, 0.0, value)
        tmp[pair, pl.ds(0, ncy, stride=2)] = value
        tmp[pair, pl.ds(1, ncy, stride=2)] = value
        for at in range(0, ny, CHUNK):
            q = slice(at, at + CHUNK)
            out[2 * pair, q] = full[2 * pair, q] + tmp[pair, q]
            out[2 * pair + 1, q] = full[2 * pair + 1, q] + tmp[pair, q]
    for cond, copy in pending:
        @pl.when(cond)
        def _(copy=copy):
            copy.wait_send()


def local(starts, material, source):
    slabs = lax.axis_size("tm")
    blocks = lax.axis_size("space")
    nx, ny, nz = source.shape
    ncx, ncy = nx // 2, ny // 2
    side = -(-CSTEPS * (slabs - 1) // 8) * 8
    whole = ncy + 2 * side
    width = ncy // slabs + 2 * side
    early = ny * 5 // 64 * 8
    f32 = functools.partial(pltpu.VMEM, dtype=jnp.float32)
    sems = lambda *shape: pltpu.SemaphoreType.DMA(shape)
    field = (nx, ny, nz)
    live = slabs - 1
    scratch = [
        pltpu.VMEM(field, jnp.int32),
        f32(field),
        f32((FSTEPS + 1, nx + 2, ny + 2 * PAD, nz)),
        f32((FSTEPS, nx + 2, early + 2 * PAD, nz)),
        f32((nx + 2, ny + 2 * PAD, nz)),
        f32((nx + 1, ny, nz)),
        *[f32(field) for _ in range(7)],
        f32((ncx + 4, whole, nz)),
        f32((8, ncx + 2, whole, nz)),
        f32((ncx + 4, whole, nz)),
        f32((ncx + 2, whole, nz)),
        f32((ncx, whole, nz)),
        f32((live, ncx + 4, width, nz)),
        f32((ncx + 2, width, nz)),
        f32((slabs, ncx, width, nz)),
        f32((ncx, width, nz)),
        f32((ncx, ncy, nz)),
        f32((ncx, ny, nz)),
        sems(3),
        sems(FSTEPS, 2), sems(FSTEPS, 2),
        sems(FSTEPS, 2), sems(FSTEPS, 2),
        sems(2), sems(2),
        sems(3, 2), sems(3, 2),
        sems(live, 2), sems(live, 2),
        sems(ncx), sems(ncx),
        sems(slabs), sems(slabs),
        sems(slabs), sems(slabs),
        sems(ncx), sems(ncx),
    ]
    hbm = pl.BlockSpec(memory_space=pl.ANY)
    result = pl.pallas_call(
        functools.partial(kernel, slabs, blocks),
        out_shape=jax.ShapeDtypeStruct(field, jnp.float32),
        in_specs=[hbm, hbm, hbm],
        out_specs=pl.BlockSpec(memory_space=pltpu.VMEM),
        scratch_shapes=scratch,
        compiler_params=pltpu.CompilerParams(
            collective_id=0, has_side_effects=True, vmem_limit_bytes=60 * 1024 * 1024
        ),
    )(starts, material, source)
    return result[None]


def solution(mesh):
    in_specs = (P("tm", "space", None, None), P("space", None, None), P("space", None, None))
    out_specs = P("tm", "space", None, None)
    return jax.shard_map(local, mesh=mesh, in_specs=in_specs, out_specs=out_specs, check_vma=False)
```

```python
import functools

import jax
import jax.numpy as jnp
from jax import lax
from jax.experimental import pallas as pl
from jax.experimental.pallas import tpu as pltpu
from jax.sharding import PartitionSpec as P

FSTEPS = 4
CSTEPS = 2
PAD = 8
CHUNK = 64

conductivity_table = (1.0, 0.72, 0.52, 0.37, 0.26, 0.18, 0.13, 0.09)
fine_step = 0.15
coarse_step = 0.3

MESH = pl.DeviceIdType.MESH


def lookup(material):
    result = jnp.zeros(material.shape, jnp.float32)
    for number in range(8):
        result = jnp.where(material == number, jnp.float32(conductivity_table[number]), result)
    return result


def kernel(slabs, blocks, starts, material, source, out, lift, mat, src, ub, ub2, kb, wx, wyl, wyh, wzl, wzh, c0, hs, full,
           kcb, cw, rub, rum, delta, rb, rm, got, last_state, ec, tmp, load_sem,
           fs, fr, f2s, f2r, ks, kr, cs, cr, chs, chr_, us, ur, vs, vr, es, er, bs, br, put_sem):
    nx, ny, nz = src.shape
    ncx, ncy = nx // 2, ny // 2
    early = ub2.shape[2] - 2 * PAD
    whole = kcb.shape[1]
    side = (whole - ncy) // 2
    rows = ncy // slabs
    width = rows + 2 * side
    late = early - 8
    live = slabs - 1
    tm = lax.axis_index("tm")
    sp = lax.axis_index("space")
    has_low = sp > 0
    has_high = sp < blocks - 1
    after = lax.rem(tm + 1, slabs)
    pending = []

    def remote(cond, src_ref, dst_ref, send, recv, **where):
        copy = pltpu.make_async_remote_copy(
            src_ref=src_ref, dst_ref=dst_ref, send_sem=send, recv_sem=recv, device_id=where, device_id_type=MESH
        )

        @pl.when(cond)
        def _():
            copy.start()

        pending.append((cond, copy))

    def arrive(cond, dst_ref, recv):
        copy = pltpu.make_async_remote_copy(
            src_ref=dst_ref, dst_ref=dst_ref, send_sem=recv, recv_sem=recv, device_id={"tm": tm}, device_id_type=MESH
        )

        @pl.when(cond)
        def _():
            copy.wait_recv()

    def halo(low_src, low_dst, high_src, high_dst, send, recv):
        remote(has_low, low_src, low_dst, send.at[0], recv.at[0], space=sp - 1)
        remote(has_high, high_src, high_dst, send.at[1], recv.at[1], space=sp + 1)

    def halo_wait(low_dst, high_dst, recv):
        arrive(has_high, low_dst, recv.at[0])
        arrive(has_low, high_dst, recv.at[1])

    barrier = pltpu.get_barrier_semaphore()

    @pl.when(has_low)
    def _():
        pl.semaphore_signal(barrier, inc=1, device_id={"space": sp - 1}, device_id_type=MESH)

    @pl.when(has_high)
    def _():
        pl.semaphore_signal(barrier, inc=1, device_id={"space": sp + 1}, device_id_type=MESH)

    for by in range(1, slabs):
        pl.semaphore_signal(barrier, inc=1, device_id={"tm": lax.rem(tm + by, slabs)}, device_id_type=MESH)

    load_mat = pltpu.make_async_copy(material, mat, load_sem.at[0])
    load_mat.start()
    load_u = pltpu.make_async_copy(starts.at[0], ub.at[0, pl.ds(1, nx), pl.ds(PAD, ny)], load_sem.at[1])
    load_u.start()
    load_src = pltpu.make_async_copy(source, src, load_sem.at[2])
    load_src.start()

    strip = jnp.zeros((PAD, nz), jnp.float32)

    def clear_rows(plane, carry):
        for step in range(FSTEPS):
            ub[step, plane, 0:PAD] = strip
            ub[step, plane, PAD + ny:PAD + ny + PAD] = strip
            ub2[step, plane, 0:PAD] = strip
            ub2[step, plane, PAD + early:PAD + early + PAD] = strip
        kb[plane, 0:PAD] = strip
        kb[plane, PAD + ny:PAD + ny + PAD] = strip
        return carry

    lax.fori_loop(1, nx + 1, clear_rows, 0)
    edge = jnp.zeros((side, nz), jnp.float32)

    def clear_sides(plane, carry):
        for ref in (kcb, rub):
            ref[plane, 0:side] = edge
            ref[plane, side + ncy:whole] = edge
        return carry

    lax.fori_loop(0, ncx + 4, clear_sides, 0)
    for plane in range(ncx + 2):
        cw[7, plane, 0:side] = edge
        cw[7, plane, side + ncy:whole] = edge
    for plane in range(ncx):
        delta[plane, 0:side] = edge
        delta[plane, side + ncy:whole] = edge

    def clear_ghosts(fine, coarse):
        for step in range(FSTEPS):
            ub[step, fine, PAD:PAD + ny] = jnp.zeros((ny, nz), jnp.float32)
            ub2[step, fine, PAD:PAD + early] = jnp.zeros((early, nz), jnp.float32)
        kb[fine, PAD:PAD + ny] = jnp.zeros((ny, nz), jnp.float32)
        for plane in (coarse, coarse + 1):
            kcb[plane] = jnp.zeros((whole, nz), jnp.float32)
            rub[plane] = jnp.zeros((whole, nz), jnp.float32)
            for slab in range(live):
                rb[slab, plane] = jnp.zeros((width, nz), jnp.float32)

    @pl.when(jnp.logical_not(has_low))
    def _():
        clear_ghosts(0, 0)
        cw[7, 0] = jnp.zeros((whole, nz), jnp.float32)

    @pl.when(jnp.logical_not(has_high))
    def _():
        clear_ghosts(nx + 1, ncx + 2)
        cw[7, ncx + 1] = jnp.zeros((whole, nz), jnp.float32)

    def conduct(plane):
        for at in range(0, ny, CHUNK):
            kb[plane + 1, PAD + at:PAD + at + CHUNK] = lookup(mat[plane, at:at + CHUNK])

    load_mat.wait()
    conduct(0)
    conduct(nx - 1)
    pl.semaphore_wait(barrier, slabs - 1 + has_low.astype(jnp.int32) + has_high.astype(jnp.int32))

    inner = pl.ds(PAD, ny)
    first_rows = pl.ds(PAD, early)
    halo(starts.at[0, 0], ub.at[0, nx + 1, inner], starts.at[0, nx - 1], ub.at[0, 0, inner], fs.at[0], fr.at[0])
    halo(kb.at[1, inner], kb.at[nx + 1, inner], kb.at[nx, inner], kb.at[0, inner], ks, kr)
    for pair in range(ncx):
        remote(True, starts.at[0, pl.ds(2 * pair, 2), pl.ds(0, early)],
               ub2.at[0, pl.ds(2 * pair + 1, 2), first_rows], us.at[pair], ur.at[pair], tm=after)

    def send_fine(step):
        halo(ub.at[step, 1, inner], ub.at[step, nx + 1, inner], ub.at[step, nx, inner], ub.at[step, 0, inner],
             fs.at[step], fr.at[step])

    def wait_fine(step):
        halo_wait(ub.at[step, nx + 1, inner], ub.at[step, 0, inner], fr.at[step])

    def send_early(step):
        halo(ub2.at[step, 1, first_rows], ub2.at[step, nx + 1, first_rows],
             ub2.at[step, nx, first_rows], ub2.at[step, 0, first_rows], f2s.at[step], f2r.at[step])

    def wait_early(step):
        halo_wait(ub2.at[step, nx + 1, first_rows], ub2.at[step, 0, first_rows], f2r.at[step])

    def conduct_loop(plane, carry):
        conduct(plane)
        return carry

    lax.fori_loop(1, nx - 1, conduct_loop, 0)
    load_src.wait()
    load_u.wait()

    def restrict_plane(ref, plane, base):
        total = ref[plane, pl.ds(base, ncy, stride=2)] + ref[plane, pl.ds(base + 1, ncy, stride=2)]
        total += ref[plane + 1, pl.ds(base, ncy, stride=2)]
        total += ref[plane + 1, pl.ds(base + 1, ncy, stride=2)]
        return total * 0.25

    core = slice(side, side + ncy)
    mid = pl.ds(side, ncy)

    def coarse_inputs():
        for plane in range(ncx):
            rub[plane + 2, core] = restrict_plane(ub.at[0], 2 * plane + 1, PAD)
            kcb[plane + 2, core] = restrict_plane(kb, 2 * plane + 1, PAD)
            cw[7, plane + 1, core] = coarse_step * restrict_plane(src, 2 * plane, 0)
        low, high = pl.ds(2, 2), pl.ds(ncx, 2)
        low_ghost, high_ghost = pl.ds(0, 2), pl.ds(ncx + 2, 2)
        halo(kcb.at[low, mid], kcb.at[high_ghost, mid], kcb.at[high, mid], kcb.at[low_ghost, mid], cs.at[0], cr.at[0])
        halo(rub.at[low, mid], rub.at[high_ghost, mid], rub.at[high, mid], rub.at[low_ghost, mid], cs.at[1], cr.at[1])
        halo(cw.at[7, 1, mid], cw.at[7, ncx + 1, mid], cw.at[7, ncx, mid], cw.at[7, 0, mid], cs.at[2], cr.at[2])

    coarse_inputs()

    def fine_weights(plane):
        half = 0.5 * fine_step
        for at in range(0, ny, CHUNK):
            r = slice(PAD + at, PAD + at + CHUNK)
            q = slice(at, at + CHUNK)
            k = kb[plane + 1, r]
            lane = lax.broadcasted_iota(jnp.int32, k.shape, 1)
            x_low = half * (k + kb[plane, r])
            x_high = half * (k + kb[plane + 2, r])
            y_low = half * (k + kb[plane + 1, PAD + at - 1:PAD + at - 1 + CHUNK])
            y_high = half * (k + kb[plane + 1, PAD + at + 1:PAD + at + 1 + CHUNK])
            first, last = lane == 0, lane == nz - 1
            z_low = half * (k + jnp.where(first, 0.0, pltpu.roll(k, 1, 1)))
            z_high = half * (k + jnp.where(last, 0.0, pltpu.roll(k, nz - 1, 1)))
            wx[plane, q] = x_low
            wx[plane + 1, q] = x_high
            wyl[plane, q] = y_low
            wyh[plane, q] = y_high
            wzl[plane, q] = jnp.where(first, 0.0, z_low)
            wzh[plane, q] = jnp.where(last, 0.0, z_high)
            c0[plane, q] = 1.0 - (x_low + x_high + y_low + y_high + z_low + z_high)
            hs[plane, q] = fine_step * src[plane, q]

    def weights_loop(plane, carry):
        fine_weights(plane)
        return carry

    lax.fori_loop(1, nx - 1, weights_loop, 0)
    halo_wait(kb.at[nx + 1, inner], kb.at[0, inner], kr)
    fine_weights(0)
    fine_weights(nx - 1)

    def fine_plane(ref, plane, count, store):
        for at in range(0, count, CHUNK):
            size = min(CHUNK, count - at)
            q = slice(at, at + size)
            r = slice(PAD + at, PAD + at + size)
            u = ref[plane + 1, r]
            total = c0[plane, q] * u + hs[plane, q]
            total += wx[plane, q] * ref[plane, r]
            total += wx[plane + 1, q] * ref[plane + 2, r]
            total += wyl[plane, q] * ref[plane + 1, PAD + at - 1:PAD + at - 1 + size]
            total += wyh[plane, q] * ref[plane + 1, PAD + at + 1:PAD + at + 1 + size]
            total += wzl[plane, q] * pltpu.roll(u, 1, 1)
            total += wzh[plane, q] * pltpu.roll(u, nz - 1, 1)
            store(plane, at, size, total)

    def sweep(ref, count, store, send):
        fine_plane(ref, 0, count, store)
        fine_plane(ref, nx - 1, count, store)
        send()

        def fine_loop(plane, carry):
            fine_plane(ref, plane, count, store)
            return carry

        lax.fori_loop(1, nx - 1, fine_loop, 0)

    def into(ref):
        def store(plane, at, size, value):
            ref[plane + 1, PAD + at:PAD + at + size] = value
        return store

    def coarse_weights():
        low_ghost, high_ghost = pl.ds(0, 2), pl.ds(ncx + 2, 2)
        halo_wait(kcb.at[high_ghost, mid], kcb.at[low_ghost, mid], cr.at[0])
        halo_wait(rub.at[high_ghost, mid], rub.at[low_ghost, mid], cr.at[1])
        halo_wait(cw.at[7, ncx + 1, mid], cw.at[7, 0, mid], cr.at[2])
        half = 0.5 * coarse_step
        near = 0.25 * half
        shape = (whole, nz)
        lane = lax.broadcasted_iota(jnp.int32, shape, 1)
        row = lax.broadcasted_iota(jnp.int32, shape, 0) - side
        first, last = lane == 0, lane == nz - 1
        low_in = jnp.logical_and(row >= 1, row < ncy)
        high_in = jnp.logical_and(row >= 0, row < ncy - 1)
        for plane in range(ncx + 2):
            k = kcb[plane + 1]
            x_low = near * (k + kcb[plane])
            x_high = near * (k + kcb[plane + 2])
            y_low = near * (k + pltpu.roll(k, 1, 0))
            y_high = near * (k + pltpu.roll(k, whole - 1, 0))
            z_low = half * (k + jnp.where(first, 0.0, pltpu.roll(k, 1, 1)))
            z_high = half * (k + jnp.where(last, 0.0, pltpu.roll(k, nz - 1, 1)))
            cw[0, plane] = 1.0 - (x_low + x_high + y_low + y_high + z_low + z_high)
            cw[1, plane] = jnp.where(has_high, x_low, 0.0) if plane == ncx + 1 else x_low
            cw[2, plane] = jnp.where(has_low, x_high, 0.0) if plane == 0 else x_high
            cw[3, plane] = jnp.where(low_in, y_low, 0.0)
            cw[4, plane] = jnp.where(high_in, y_high, 0.0)
            cw[5, plane] = jnp.where(first, 0.0, z_low)
            cw[6, plane] = jnp.where(last, 0.0, z_high)

    def coarse_plane(ref, plane, pick, offset):
        v = ref[plane + 1]
        at = plane + offset
        total = cw[0, at, pick] * v + cw[7, at, pick]
        total += cw[1, at, pick] * ref[plane]
        total += cw[2, at, pick] * ref[plane + 2]
        total += cw[3, at, pick] * pltpu.roll(v, 1, 0)
        total += cw[4, at, pick] * pltpu.roll(v, v.shape[0] - 1, 0)
        total += cw[5, at, pick] * pltpu.roll(v, 1, 1)
        total += cw[6, at, pick] * pltpu.roll(v, nz - 1, 1)
        return total

    def coarse_map(ref, middle, pick, store):
        for plane in range(ncx + 2):
            middle[plane] = coarse_plane(ref, plane, pick, 0)
        for plane in range(ncx):
            store(plane, coarse_plane(middle, plane, pick, 1))

    for step in range(FSTEPS):
        wait_fine(step)

        def send(step=step):
            if step < FSTEPS - 1:
                send_fine(step + 1)

        sweep(ub.at[step], ny, into(ub.at[step + 1]), send)
        if step == FSTEPS - 3:
            coarse_weights()
        if step == FSTEPS - 2:

            def keep_minus(plane, value):
                delta[plane] = jnp.where(tm > 0, -value, 0.0)

            coarse_map(rub, rum, slice(0, whole), keep_minus)

    for plane in range(ncx):
        delta[plane, core] = delta[plane, core] + restrict_plane(ub.at[FSTEPS], 2 * plane + 1, PAD)
    for to in range(slabs):
        remote(tm != to, delta.at[:, pl.ds(rows * to, width)], got.at[tm], vs.at[to], vr.at[tm], tm=to)
    for pair in range(ncx):
        remote(True, ub.at[FSTEPS, pl.ds(2 * pair + 1, 2), pl.ds(PAD + late, ny - late)],
               full.at[pl.ds(2 * pair, 2), pl.ds(late, ny - late)], bs.at[pair], br.at[pair], tm=after)

    mine = pl.ds(pl.multiple_of(rows * tm, 8), width)

    def end_state(slab):
        arrive(tm != slab, got.at[slab], vr.at[slab])

        @pl.when(tm == slab)
        def _():
            for plane in range(ncx):
                got[slab, plane] = delta[plane, mine]

    def send_chain(slab):
        halo(rb.at[slab, pl.ds(2, 2)], rb.at[slab, pl.ds(ncx + 2, 2)], rb.at[slab, pl.ds(ncx, 2)],
             rb.at[slab, pl.ds(0, 2)], chs.at[slab], chr_.at[slab])

    own_rows = pl.ds(pl.multiple_of(rows * tm, 8), rows)

    def chain(slab):
        end_state(slab + 1)
        halo_wait(rb.at[slab, pl.ds(ncx + 2, 2)], rb.at[slab, pl.ds(0, 2)], chr_.at[slab])
        to = (slab + 2) % slabs

        if slab + 1 < live:
            def store(plane, value):
                rb[slab + 1, plane + 2] = value + got[slab + 1, plane]

            coarse_map(rb.at[slab], rm, mine, store)
            send_chain(slab + 1)
            result = rb.at[slab + 1, pl.ds(2, ncx)]
        else:
            def store(plane, value):
                last_state[plane] = value + got[slab + 1, plane]

            coarse_map(rb.at[slab], rm, mine, store)
            result = last_state
        remote(tm != to, result.at[:, pl.ds(side, rows)], ec.at[:, own_rows], es.at[slab], er.at[tm], tm=to)

        @pl.when(tm == to)
        def _():
            for plane in range(ncx):
                ec[plane, own_rows] = result[plane, side:side + rows]

    for pair in range(ncx):
        arrive(True, ub2.at[0, pl.ds(2 * pair + 1, 2), first_rows], ur.at[pair])
    send_early(0)

    def early_step(step):
        wait_early(step)
        if step < FSTEPS - 1:
            sweep(ub2.at[step], early, into(ub2.at[step + 1]), lambda: send_early(step + 1))
        else:
            def store(plane, at, size, value):
                full[plane, at:at + size] = value

            sweep(ub2.at[step], late, store, lambda: None)

    early_step(0)
    end_state(0)
    for plane in range(ncx):
        rb[0, plane + 2] = got[0, plane]
    send_chain(0)
    for turn in range(max(FSTEPS - 1, live)):
        if turn + 1 < FSTEPS:
            early_step(turn + 1)
        if turn < live:
            chain(turn)

    @pl.when(tm == 1)
    def _():
        for plane in range(ncx):
            ec[plane] = jnp.zeros((ncy, nz), jnp.float32)

    stored = []
    for by in range(slabs):
        arrive(jnp.logical_and(tm != 1, tm != by), ec.at[:, pl.ds(rows * by, rows)], er.at[by])
    for pair in range(ncx):
        arrive(True, full.at[pl.ds(2 * pair, 2), pl.ds(late, ny - late)], br.at[pair])
        value = ec[pair] - restrict_plane(full, 2 * pair, 0)
        value = jnp.where(tm == 1, 0.0, value)
        tmp[pair, pl.ds(0, ncy, stride=2)] = value
        tmp[pair, pl.ds(1, ncy, stride=2)] = value
        put_lift = pltpu.make_async_copy(tmp.at[pair], lift.at[pair], put_sem.at[1, pair])
        put_lift.start()
        put_out = pltpu.make_async_copy(full.at[pl.ds(2 * pair, 2)], out.at[pl.ds(2 * pair, 2)], put_sem.at[0, pair])
        put_out.start()
        stored += [put_lift, put_out]
    for copy in stored:
        copy.wait()
    for cond, copy in pending:
        @pl.when(cond)
        def _(copy=copy):
            copy.wait_send()


def local(starts, material, source):
    slabs = lax.axis_size("tm")
    blocks = lax.axis_size("space")
    nx, ny, nz = source.shape
    ncx, ncy = nx // 2, ny // 2
    side = -(-CSTEPS * (slabs - 1) // 8) * 8
    whole = ncy + 2 * side
    width = ncy // slabs + 2 * side
    early = ny * 6 // 64 * 8
    f32 = functools.partial(pltpu.VMEM, dtype=jnp.float32)
    sems = lambda *shape: pltpu.SemaphoreType.DMA(shape)
    field = (nx, ny, nz)
    live = slabs - 1
    scratch = [
        pltpu.VMEM(field, jnp.int32),
        f32(field),
        f32((FSTEPS + 1, nx + 2, ny + 2 * PAD, nz)),
        f32((FSTEPS, nx + 2, early + 2 * PAD, nz)),
        f32((nx + 2, ny + 2 * PAD, nz)),
        f32((nx + 1, ny, nz)),
        *[f32(field) for _ in range(7)],
        f32((ncx + 4, whole, nz)),
        f32((8, ncx + 2, whole, nz)),
        f32((ncx + 4, whole, nz)),
        f32((ncx + 2, whole, nz)),
        f32((ncx, whole, nz)),
        f32((live, ncx + 4, width, nz)),
        f32((ncx + 2, width, nz)),
        f32((slabs, ncx, width, nz)),
        f32((ncx, width, nz)),
        f32((ncx, ncy, nz)),
        f32((ncx, ny, nz)),
        sems(3),
        sems(FSTEPS, 2), sems(FSTEPS, 2),
        sems(FSTEPS, 2), sems(FSTEPS, 2),
        sems(2), sems(2),
        sems(3, 2), sems(3, 2),
        sems(live, 2), sems(live, 2),
        sems(ncx), sems(ncx),
        sems(slabs), sems(slabs),
        sems(slabs), sems(slabs),
        sems(ncx), sems(ncx),
        sems(2, ncx),
    ]
    hbm = pl.BlockSpec(memory_space=pl.ANY)
    fine, lift = pl.pallas_call(
        functools.partial(kernel, slabs, blocks),
        out_shape=[jax.ShapeDtypeStruct(field, jnp.float32), jax.ShapeDtypeStruct((ncx, ny, nz), jnp.float32)],
        in_specs=[hbm, hbm, hbm],
        out_specs=[hbm, hbm],
        scratch_shapes=scratch,
        compiler_params=pltpu.CompilerParams(
            collective_id=0, has_side_effects=True, vmem_limit_bytes=60 * 1024 * 1024
        ),
    )(starts, material, source)
    return (fine.reshape(ncx, 2, ny, nz) + lift[:, None]).reshape(1, nx, ny, nz)


def solution(mesh):
    in_specs = (P("tm", "space", None, None), P("space", None, None), P("space", None, None))
    out_specs = P("tm", "space", None, None)
    return jax.shard_map(local, mesh=mesh, in_specs=in_specs, out_specs=out_specs, check_vma=False)
```

```python
import functools

import jax
import jax.numpy as jnp
from jax import lax
from jax.experimental import pallas as pl
from jax.experimental.pallas import tpu as pltpu
from jax.sharding import PartitionSpec as P

FSTEPS = 4
CSTEPS = 2
PAD = 8
CHUNK = 64

conductivity_table = (1.0, 0.72, 0.52, 0.37, 0.26, 0.18, 0.13, 0.09)
fine_step = 0.15
coarse_step = 0.3

MESH = pl.DeviceIdType.MESH


def lookup(material):
    result = jnp.zeros(material.shape, jnp.float32)
    for number in range(8):
        result = jnp.where(material == number, jnp.float32(conductivity_table[number]), result)
    return result


def kernel(slabs, blocks, starts, material, source, out, lift, mat, src, ub, ub2, kb, wx, wyl, wyh, wzl, wzh, c0, hs, full,
           kcb, cw, rub, rum, delta, rb, rm, got, last_state, ec, ends, tmp, load_sem,
           fs, fr, f2s, f2r, ks, kr, cs, cr, chs, chr_, us, ur, vs, vr, es, er, bs, br, put_sem):
    nx, ny, nz = src.shape
    ncx, ncy = nx // 2, ny // 2
    early = ub2.shape[2] - 2 * PAD
    whole = kcb.shape[1]
    side = (whole - ncy) // 2
    rows = ncy // slabs
    width = rows + 2 * side
    late = early - 8
    live = slabs - 1
    tm = lax.axis_index("tm")
    sp = lax.axis_index("space")
    has_low = sp > 0
    has_high = sp < blocks - 1
    after = lax.rem(tm + 1, slabs)
    pending = []

    def remote(cond, src_ref, dst_ref, send, recv, **where):
        copy = pltpu.make_async_remote_copy(
            src_ref=src_ref, dst_ref=dst_ref, send_sem=send, recv_sem=recv, device_id=where, device_id_type=MESH
        )

        @pl.when(cond)
        def _():
            copy.start()

        pending.append((cond, copy))

    def arrive(cond, dst_ref, recv):
        copy = pltpu.make_async_remote_copy(
            src_ref=dst_ref, dst_ref=dst_ref, send_sem=recv, recv_sem=recv, device_id={"tm": tm}, device_id_type=MESH
        )

        @pl.when(cond)
        def _():
            copy.wait_recv()

    def halo(low_src, low_dst, high_src, high_dst, send, recv):
        remote(has_low, low_src, low_dst, send.at[0], recv.at[0], space=sp - 1)
        remote(has_high, high_src, high_dst, send.at[1], recv.at[1], space=sp + 1)

    def halo_wait(low_dst, high_dst, recv):
        arrive(has_high, low_dst, recv.at[0])
        arrive(has_low, high_dst, recv.at[1])

    barrier = pltpu.get_barrier_semaphore()

    @pl.when(has_low)
    def _():
        pl.semaphore_signal(barrier, inc=1, device_id={"space": sp - 1}, device_id_type=MESH)

    @pl.when(has_high)
    def _():
        pl.semaphore_signal(barrier, inc=1, device_id={"space": sp + 1}, device_id_type=MESH)

    for by in range(1, slabs):
        pl.semaphore_signal(barrier, inc=1, device_id={"tm": lax.rem(tm + by, slabs)}, device_id_type=MESH)

    load_mat = pltpu.make_async_copy(material, mat, load_sem.at[0])
    load_mat.start()
    load_u = pltpu.make_async_copy(starts.at[0], ub.at[0, pl.ds(1, nx), pl.ds(PAD, ny)], load_sem.at[1])
    load_u.start()
    load_src = pltpu.make_async_copy(source, src, load_sem.at[2])
    load_src.start()

    strip = jnp.zeros((PAD, nz), jnp.float32)

    def clear_rows(plane, carry):
        for step in range(FSTEPS):
            ub[step, plane, 0:PAD] = strip
            ub[step, plane, PAD + ny:PAD + ny + PAD] = strip
            ub2[step, plane, 0:PAD] = strip
            ub2[step, plane, PAD + early:PAD + early + PAD] = strip
        kb[plane, 0:PAD] = strip
        kb[plane, PAD + ny:PAD + ny + PAD] = strip
        return carry

    lax.fori_loop(1, nx + 1, clear_rows, 0)
    edge = jnp.zeros((side, nz), jnp.float32)

    def clear_sides(plane, carry):
        for ref in (kcb, rub):
            ref[plane, 0:side] = edge
            ref[plane, side + ncy:whole] = edge
        return carry

    lax.fori_loop(0, ncx + 4, clear_sides, 0)
    for plane in range(ncx + 2):
        cw[7, plane, 0:side] = edge
        cw[7, plane, side + ncy:whole] = edge
    for plane in range(ncx):
        delta[plane, 0:side] = edge
        delta[plane, side + ncy:whole] = edge

    def clear_ghosts(fine, coarse):
        for step in range(FSTEPS):
            ub[step, fine, PAD:PAD + ny] = jnp.zeros((ny, nz), jnp.float32)
            ub2[step, fine, PAD:PAD + early] = jnp.zeros((early, nz), jnp.float32)
        kb[fine, PAD:PAD + ny] = jnp.zeros((ny, nz), jnp.float32)
        for plane in (coarse, coarse + 1):
            kcb[plane] = jnp.zeros((whole, nz), jnp.float32)
            rub[plane] = jnp.zeros((whole, nz), jnp.float32)
            for slab in range(live):
                rb[slab, plane] = jnp.zeros((width, nz), jnp.float32)

    @pl.when(jnp.logical_not(has_low))
    def _():
        clear_ghosts(0, 0)
        cw[7, 0] = jnp.zeros((whole, nz), jnp.float32)

    @pl.when(jnp.logical_not(has_high))
    def _():
        clear_ghosts(nx + 1, ncx + 2)
        cw[7, ncx + 1] = jnp.zeros((whole, nz), jnp.float32)

    def conduct(plane):
        for at in range(0, ny, CHUNK):
            kb[plane + 1, PAD + at:PAD + at + CHUNK] = lookup(mat[plane, at:at + CHUNK])

    load_mat.wait()
    conduct(0)
    conduct(nx - 1)
    pl.semaphore_wait(barrier, slabs - 1 + has_low.astype(jnp.int32) + has_high.astype(jnp.int32))

    inner = pl.ds(PAD, ny)
    first_rows = pl.ds(PAD, early)
    halo(starts.at[0, 0], ub.at[0, nx + 1, inner], starts.at[0, nx - 1], ub.at[0, 0, inner], fs.at[0], fr.at[0])
    halo(kb.at[1, inner], kb.at[nx + 1, inner], kb.at[nx, inner], kb.at[0, inner], ks, kr)
    for pair in range(ncx):
        remote(True, starts.at[0, pl.ds(2 * pair, 2), pl.ds(0, early)],
               ub2.at[0, pl.ds(2 * pair + 1, 2), first_rows], us.at[pair], ur.at[pair], tm=after)

    def send_fine(step):
        halo(ub.at[step, 1, inner], ub.at[step, nx + 1, inner], ub.at[step, nx, inner], ub.at[step, 0, inner],
             fs.at[step], fr.at[step])

    def wait_fine(step):
        halo_wait(ub.at[step, nx + 1, inner], ub.at[step, 0, inner], fr.at[step])

    def send_early(step):
        halo(ub2.at[step, 1, first_rows], ub2.at[step, nx + 1, first_rows],
             ub2.at[step, nx, first_rows], ub2.at[step, 0, first_rows], f2s.at[step], f2r.at[step])

    def wait_early(step):
        halo_wait(ub2.at[step, nx + 1, first_rows], ub2.at[step, 0, first_rows], f2r.at[step])

    def conduct_loop(plane, carry):
        conduct(plane)
        return carry

    lax.fori_loop(1, nx - 1, conduct_loop, 0)
    load_src.wait()
    load_u.wait()

    def restrict_plane(ref, plane, base):
        total = ref[plane, pl.ds(base, ncy, stride=2)] + ref[plane, pl.ds(base + 1, ncy, stride=2)]
        total += ref[plane + 1, pl.ds(base, ncy, stride=2)]
        total += ref[plane + 1, pl.ds(base + 1, ncy, stride=2)]
        return total * 0.25

    core = slice(side, side + ncy)
    mid = pl.ds(side, ncy)

    def coarse_inputs():
        for plane in range(ncx):
            rub[plane + 2, core] = restrict_plane(ub.at[0], 2 * plane + 1, PAD)
            kcb[plane + 2, core] = restrict_plane(kb, 2 * plane + 1, PAD)
            cw[7, plane + 1, core] = coarse_step * restrict_plane(src, 2 * plane, 0)
        low, high = pl.ds(2, 2), pl.ds(ncx, 2)
        low_ghost, high_ghost = pl.ds(0, 2), pl.ds(ncx + 2, 2)
        halo(kcb.at[low, mid], kcb.at[high_ghost, mid], kcb.at[high, mid], kcb.at[low_ghost, mid], cs.at[0], cr.at[0])
        halo(rub.at[low, mid], rub.at[high_ghost, mid], rub.at[high, mid], rub.at[low_ghost, mid], cs.at[1], cr.at[1])
        halo(cw.at[7, 1, mid], cw.at[7, ncx + 1, mid], cw.at[7, ncx, mid], cw.at[7, 0, mid], cs.at[2], cr.at[2])

    coarse_inputs()

    def fine_weights(plane):
        half = 0.5 * fine_step
        for at in range(0, ny, CHUNK):
            r = slice(PAD + at, PAD + at + CHUNK)
            q = slice(at, at + CHUNK)
            k = kb[plane + 1, r]
            lane = lax.broadcasted_iota(jnp.int32, k.shape, 1)
            x_low = half * (k + kb[plane, r])
            x_high = half * (k + kb[plane + 2, r])
            y_low = half * (k + kb[plane + 1, PAD + at - 1:PAD + at - 1 + CHUNK])
            y_high = half * (k + kb[plane + 1, PAD + at + 1:PAD + at + 1 + CHUNK])
            first, last = lane == 0, lane == nz - 1
            z_low = half * (k + jnp.where(first, 0.0, pltpu.roll(k, 1, 1)))
            z_high = half * (k + jnp.where(last, 0.0, pltpu.roll(k, nz - 1, 1)))
            wx[plane, q] = x_low
            wx[plane + 1, q] = x_high
            wyl[plane, q] = y_low
            wyh[plane, q] = y_high
            wzl[plane, q] = jnp.where(first, 0.0, z_low)
            wzh[plane, q] = jnp.where(last, 0.0, z_high)
            c0[plane, q] = 1.0 - (x_low + x_high + y_low + y_high + z_low + z_high)
            hs[plane, q] = fine_step * src[plane, q]

    def weights_loop(plane, carry):
        fine_weights(plane)
        return carry

    lax.fori_loop(1, nx - 1, weights_loop, 0)
    halo_wait(kb.at[nx + 1, inner], kb.at[0, inner], kr)
    fine_weights(0)
    fine_weights(nx - 1)

    def fine_plane(ref, plane, count, store):
        for at in range(0, count, CHUNK):
            size = min(CHUNK, count - at)
            q = slice(at, at + size)
            r = slice(PAD + at, PAD + at + size)
            u = ref[plane + 1, r]
            total = c0[plane, q] * u + hs[plane, q]
            total += wx[plane, q] * ref[plane, r]
            total += wx[plane + 1, q] * ref[plane + 2, r]
            total += wyl[plane, q] * ref[plane + 1, PAD + at - 1:PAD + at - 1 + size]
            total += wyh[plane, q] * ref[plane + 1, PAD + at + 1:PAD + at + 1 + size]
            total += wzl[plane, q] * pltpu.roll(u, 1, 1)
            total += wzh[plane, q] * pltpu.roll(u, nz - 1, 1)
            store(plane, at, size, total)

    def sweep(ref, count, store, send):
        fine_plane(ref, 0, count, store)
        fine_plane(ref, nx - 1, count, store)
        send()

        def fine_loop(plane, carry):
            fine_plane(ref, plane, count, store)
            return carry

        lax.fori_loop(1, nx - 1, fine_loop, 0)

    def into(ref):
        def store(plane, at, size, value):
            ref[plane + 1, PAD + at:PAD + at + size] = value
        return store

    def coarse_weights():
        low_ghost, high_ghost = pl.ds(0, 2), pl.ds(ncx + 2, 2)
        halo_wait(kcb.at[high_ghost, mid], kcb.at[low_ghost, mid], cr.at[0])
        halo_wait(rub.at[high_ghost, mid], rub.at[low_ghost, mid], cr.at[1])
        halo_wait(cw.at[7, ncx + 1, mid], cw.at[7, 0, mid], cr.at[2])
        half = 0.5 * coarse_step
        near = 0.25 * half
        shape = (whole, nz)
        lane = lax.broadcasted_iota(jnp.int32, shape, 1)
        row = lax.broadcasted_iota(jnp.int32, shape, 0) - side
        first, last = lane == 0, lane == nz - 1
        low_in = jnp.logical_and(row >= 1, row < ncy)
        high_in = jnp.logical_and(row >= 0, row < ncy - 1)
        for plane in range(ncx + 2):
            k = kcb[plane + 1]
            x_low = near * (k + kcb[plane])
            x_high = near * (k + kcb[plane + 2])
            y_low = near * (k + pltpu.roll(k, 1, 0))
            y_high = near * (k + pltpu.roll(k, whole - 1, 0))
            z_low = half * (k + jnp.where(first, 0.0, pltpu.roll(k, 1, 1)))
            z_high = half * (k + jnp.where(last, 0.0, pltpu.roll(k, nz - 1, 1)))
            cw[0, plane] = 1.0 - (x_low + x_high + y_low + y_high + z_low + z_high)
            cw[1, plane] = jnp.where(has_high, x_low, 0.0) if plane == ncx + 1 else x_low
            cw[2, plane] = jnp.where(has_low, x_high, 0.0) if plane == 0 else x_high
            cw[3, plane] = jnp.where(low_in, y_low, 0.0)
            cw[4, plane] = jnp.where(high_in, y_high, 0.0)
            cw[5, plane] = jnp.where(first, 0.0, z_low)
            cw[6, plane] = jnp.where(last, 0.0, z_high)

    def coarse_plane(ref, plane, pick, offset):
        v = ref[plane + 1]
        at = plane + offset
        total = cw[0, at, pick] * v + cw[7, at, pick]
        total += cw[1, at, pick] * ref[plane]
        total += cw[2, at, pick] * ref[plane + 2]
        total += cw[3, at, pick] * pltpu.roll(v, 1, 0)
        total += cw[4, at, pick] * pltpu.roll(v, v.shape[0] - 1, 0)
        total += cw[5, at, pick] * pltpu.roll(v, 1, 1)
        total += cw[6, at, pick] * pltpu.roll(v, nz - 1, 1)
        return total

    def coarse_map(ref, middle, pick, store):
        for plane in range(ncx + 2):
            middle[plane] = coarse_plane(ref, plane, pick, 0)
        for plane in range(ncx):
            store(plane, coarse_plane(middle, plane, pick, 1))

    for step in range(FSTEPS):
        wait_fine(step)

        def send(step=step):
            if step < FSTEPS - 1:
                send_fine(step + 1)

        sweep(ub.at[step], ny, into(ub.at[step + 1]), send)
        if step == FSTEPS - 3:
            coarse_weights()
        if step == FSTEPS - 2:

            def keep_minus(plane, value):
                delta[plane] = jnp.where(tm > 0, -value, 0.0)

            coarse_map(rub, rum, slice(0, whole), keep_minus)

    for plane in range(ncx):
        delta[plane, core] = delta[plane, core] + restrict_plane(ub.at[FSTEPS], 2 * plane + 1, PAD)
    for to in range(slabs):
        remote(tm != to, delta.at[:, pl.ds(rows * to, width)], got.at[tm], vs.at[to], vr.at[tm], tm=to)

    mine = pl.ds(pl.multiple_of(rows * tm, 8), width)

    def end_state(slab):
        arrive(tm != slab, got.at[slab], vr.at[slab])

        @pl.when(tm == slab)
        def _():
            for plane in range(ncx):
                got[slab, plane] = delta[plane, mine]

    def send_chain(slab):
        halo(rb.at[slab, pl.ds(2, 2)], rb.at[slab, pl.ds(ncx + 2, 2)], rb.at[slab, pl.ds(ncx, 2)],
             rb.at[slab, pl.ds(0, 2)], chs.at[slab], chr_.at[slab])

    own_rows = pl.ds(pl.multiple_of(rows * tm, 8), rows)

    def chain(slab):
        end_state(slab + 1)
        halo_wait(rb.at[slab, pl.ds(ncx + 2, 2)], rb.at[slab, pl.ds(0, 2)], chr_.at[slab])
        to = (slab + 2) % slabs

        if slab + 1 < live:
            def store(plane, value):
                rb[slab + 1, plane + 2] = value + got[slab + 1, plane]

            coarse_map(rb.at[slab], rm, mine, store)
            send_chain(slab + 1)
            result = rb.at[slab + 1, pl.ds(2, ncx)]
        else:
            def store(plane, value):
                last_state[plane] = value + got[slab + 1, plane]

            coarse_map(rb.at[slab], rm, mine, store)
            result = last_state
        remote(tm != to, result.at[:, pl.ds(side, rows)], ec.at[:, own_rows], es.at[slab], er.at[tm], tm=to)

        @pl.when(tm == to)
        def _():
            for plane in range(ncx):
                ec[plane, own_rows] = result[plane, side:side + rows]

    for pair in range(ncx):
        arrive(True, ub2.at[0, pl.ds(2 * pair + 1, 2), first_rows], ur.at[pair])
    send_early(0)

    def early_step(step):
        wait_early(step)
        if step < FSTEPS - 1:
            sweep(ub2.at[step], early, into(ub2.at[step + 1]), lambda: send_early(step + 1))
        else:
            def store(plane, at, size, value):
                full[plane, at:at + size] = value

            sweep(ub2.at[step], late, store, lambda: None)

    early_step(0)
    end_state(0)
    for plane in range(ncx):
        rb[0, plane + 2] = got[0, plane]
    send_chain(0)
    for pair in range(ncx):
        remote(True, ub.at[FSTEPS, pl.ds(2 * pair + 1, 2), pl.ds(PAD + late, ny - late)],
               full.at[pl.ds(2 * pair, 2), pl.ds(late, ny - late)], bs.at[pair], br.at[pair], tm=after)
    for turn in range(max(FSTEPS - 1, live)):
        if turn + 1 < FSTEPS:
            early_step(turn + 1)
        if turn < live:
            chain(turn)

    @pl.when(tm == 1)
    def _():
        for plane in range(ncx):
            ec[plane] = jnp.zeros((ncy, nz), jnp.float32)

    stored = []
    for pair in range(ncx):
        arrive(True, full.at[pl.ds(2 * pair, 2), pl.ds(late, ny - late)], br.at[pair])
        put_out = pltpu.make_async_copy(full.at[pl.ds(2 * pair, 2)], out.at[pl.ds(2 * pair, 2)], put_sem.at[0, pair])
        put_out.start()
        stored.append(put_out)
        ends[pair] = restrict_plane(full, 2 * pair, 0)
    for by in range(slabs):
        arrive(jnp.logical_and(tm != 1, tm != by), ec.at[:, pl.ds(rows * by, rows)], er.at[by])
    for pair in range(ncx):
        value = jnp.where(tm == 1, 0.0, ec[pair] - ends[pair])
        tmp[pair, pl.ds(0, ncy, stride=2)] = value
        tmp[pair, pl.ds(1, ncy, stride=2)] = value
        put_lift = pltpu.make_async_copy(tmp.at[pair], lift.at[pair], put_sem.at[1, pair])
        put_lift.start()
        stored.append(put_lift)
    for copy in stored:
        copy.wait()
    for cond, copy in pending:
        @pl.when(cond)
        def _(copy=copy):
            copy.wait_send()


def local(starts, material, source):
    slabs = lax.axis_size("tm")
    blocks = lax.axis_size("space")
    nx, ny, nz = source.shape
    ncx, ncy = nx // 2, ny // 2
    side = -(-CSTEPS * (slabs - 1) // 8) * 8
    whole = ncy + 2 * side
    width = ncy // slabs + 2 * side
    early = ny * 6 // 64 * 8
    f32 = functools.partial(pltpu.VMEM, dtype=jnp.float32)
    sems = lambda *shape: pltpu.SemaphoreType.DMA(shape)
    field = (nx, ny, nz)
    live = slabs - 1
    scratch = [
        pltpu.VMEM(field, jnp.int32),
        f32(field),
        f32((FSTEPS + 1, nx + 2, ny + 2 * PAD, nz)),
        f32((FSTEPS, nx + 2, early + 2 * PAD, nz)),
        f32((nx + 2, ny + 2 * PAD, nz)),
        f32((nx + 1, ny, nz)),
        *[f32(field) for _ in range(7)],
        f32((ncx + 4, whole, nz)),
        f32((8, ncx + 2, whole, nz)),
        f32((ncx + 4, whole, nz)),
        f32((ncx + 2, whole, nz)),
        f32((ncx, whole, nz)),
        f32((live, ncx + 4, width, nz)),
        f32((ncx + 2, width, nz)),
        f32((slabs, ncx, width, nz)),
        f32((ncx, width, nz)),
        f32((ncx, ncy, nz)),
        f32((ncx, ncy, nz)),
        f32((ncx, ny, nz)),
        sems(3),
        sems(FSTEPS, 2), sems(FSTEPS, 2),
        sems(FSTEPS, 2), sems(FSTEPS, 2),
        sems(2), sems(2),
        sems(3, 2), sems(3, 2),
        sems(live, 2), sems(live, 2),
        sems(ncx), sems(ncx),
        sems(slabs), sems(slabs),
        sems(slabs), sems(slabs),
        sems(ncx), sems(ncx),
        sems(2, ncx),
    ]
    hbm = pl.BlockSpec(memory_space=pl.ANY)
    fine, lift = pl.pallas_call(
        functools.partial(kernel, slabs, blocks),
        out_shape=[jax.ShapeDtypeStruct(field, jnp.float32), jax.ShapeDtypeStruct((ncx, ny, nz), jnp.float32)],
        in_specs=[hbm, hbm, hbm],
        out_specs=[hbm, hbm],
        scratch_shapes=scratch,
        compiler_params=pltpu.CompilerParams(
            collective_id=0, has_side_effects=True, vmem_limit_bytes=60 * 1024 * 1024
        ),
    )(starts, material, source)
    return (fine.reshape(ncx, 2, ny, nz) + lift[:, None]).reshape(1, nx, ny, nz)


def solution(mesh):
    in_specs = (P("tm", "space", None, None), P("space", None, None), P("space", None, None))
    out_specs = P("tm", "space", None, None)
    return jax.shard_map(local, mesh=mesh, in_specs=in_specs, out_specs=out_specs, check_vma=False)
```
